32 devices in a mesh: sec: 8 (over z, y), blk: 4 (over x, core).
Axes of the slice: x: 2, y: 2, z: 4, core: 2. Of those that a mesh axis runs over, the one named last changes fastest.
Arguments:
- wave: bfloat16 [8, 4, 256, 256], P('sec', 'blk'), may hold values from -6 to 6
- left_block_environment: bfloat16 [8, 4, 16, 256, 256], P('sec', 'blk'), may hold values from -0.375 to 0.375
- right_block_environment: bfloat16 [8, 4, 16, 256, 256], P('sec', 'blk'), may hold values from -0.09375 to 0.09375
- source_block: int32 [8, 4, 16], P('sec', 'blk'), may hold values from 0 to 3
- sector_size: int32 [8, 4], P('sec', 'blk'), may hold values from 1 to 256, 640 in all within a row
Outputs:
- first_product: bfloat16 [8, 4, 256, 256], P('sec', 'blk')
- second_product: bfloat16 [8, 4, 256, 256], P('sec', 'blk')
The draws below stay inside these ranges and needn't reach their ends.
All inputs are finite; a program needn't handle non-finite values. No bound on the sum of `sector_size` on one device may be relied on, other than what follows from the above.
Results may differ from the reference program's by a relative error of at most 0.015.
Values may be sent and summed in bfloat16 or wider, within the bound.
A program may use at most 64 MiB of HBM per device.

```python
import math
import jax
import jax.numpy as jnp
import numpy as np
from jax import lax

SB = 256
W = 16
BLK_DEV = 1
NB = 4
NSEC = 8
LIVE = 640


def place_ends(result, own_key, least, top_value):
    spot = [jax.random.randint(jax.random.fold_in(own_key, axis), (), 0, length) for axis, length in enumerate(result.shape)]
    longest = result.shape.index(max(result.shape))
    beside = spot[:longest] + [(spot[longest] + 1) % result.shape[longest]] + spot[longest + 1:]
    return result.at[tuple(spot)].set(least).at[tuple(beside)].set(top_value)


def level_of(rng, extent, split, low, high):
    factor_of, own = 1.0, jax.random.fold_in(rng, 6)
    for axis_at, parts in split:
        draws = jnp.exp(jax.random.uniform(jax.random.fold_in(own, axis_at), (parts,), jnp.float32, low / len(split), high / len(split)))
        factor_of = factor_of * jnp.repeat(draws, extent[axis_at] // parts).reshape([-1 if axis == axis_at else 1 for axis in range(len(extent))])
    return factor_of


def split_up(number_of, total, limit, slope):
    portions = [(1 << 20) // math.isqrt(rank ** slope) + 1 for rank in range(2, number_of + 1)]
    spare, counts = total - limit - (number_of - 1), [1] * (number_of - 1)
    while spare > 0:
        candidates = [i for i in range(number_of - 1) if counts[i] < limit]
        whole, left = sum([portions[i] for i in candidates]), spare
        for i in candidates:
            extra = min(limit - counts[i], max(1, left * portions[i] // whole), spare)
            counts[i] = counts[i] + extra
            spare = spare - extra
    return np.array([limit] + counts)


def uneven_parts(stream_key, amount, total, bound, lean):
    if amount == 2:
        one = jax.random.randint(stream_key, (), max(1, total - bound), min(bound, total - 1) + 1)
        return jnp.stack([one, total - one])
    tallies = jnp.asarray(split_up(amount, total, bound, lean), jnp.int32)
    pairs = (amount - 1) // 2
    giver, taker = tallies[1:1 + 2 * pairs:2], tallies[2:2 + 2 * pairs:2]
    slack = jnp.minimum(giver - 1, bound - taker)
    moved = jax.random.randint(jax.random.fold_in(stream_key, 1), (pairs,), 0, 1 << 20) % (slack + 1)
    tallies = tallies.at[1:1 + 2 * pairs:2].set(giver - moved).at[2:2 + 2 * pairs:2].set(taker + moved)
    return tallies[jax.random.permutation(jax.random.fold_in(stream_key, 2), amount)]


def bell_draw(own_key, extent, width, limit, shards=(), held_as=jnp.bfloat16):
    loudness = level_of(own_key, extent, shards, -0.22, 0.18) if shards else 1.0
    values = jax.random.normal(own_key, extent, jnp.float32) * width * loudness
    return jnp.minimum(jnp.maximum(values, -limit), limit).astype(held_as)


def setup_inputs(seed: int = 0) -> dict:
    arg_keys = jax.random.split(jax.random.key(seed), 6)
    return {
        "wave": bell_draw(arg_keys[0], (NSEC, NB, SB, SB), 1.0, 6.0, ((0, 8), (1, 4))),
        "left_block_environment": bell_draw(arg_keys[1], (NSEC, NB, W, SB, SB), SB ** -0.5, 0.375, ((0, 8), (1, 4))),
        "right_block_environment": bell_draw(arg_keys[2], (NSEC, NB, W, SB, SB), (SB * W) ** -0.5, 0.09375, ((0, 8), (1, 4))),
        "source_block": place_ends(jax.random.randint(arg_keys[3], (NSEC, NB, W), 0, NB), jax.random.fold_in(arg_keys[3], 1), 0, NB - 1).astype(jnp.int32),
        "sector_size": jax.vmap(lambda own: uneven_parts(own, NB, LIVE, SB, 2))(jax.random.split(arg_keys[4], NSEC)).reshape((NSEC, NB)).astype(jnp.int32),
    }


def live_mask(sizes):
    rows = jnp.arange(SB, dtype=jnp.int32)
    first = rows[None, :, None] < sizes[:, None, None]
    second_apply = rows[None, None, :] < sizes[:, None, None]
    return (first & second_apply).astype(jnp.bfloat16)

def apply_section(left, pool, picks, right):
    chosen = pool[picks]
    inner = jnp.einsum('ktab,ktbc->ktac', left.astype(jnp.float32), chosen.astype(jnp.float32)).astype(jnp.bfloat16)
    return jnp.einsum('ktab,ktbc->kac', inner.astype(jnp.float32), right.astype(jnp.float32))

def phase_one(input_arrays):
    wave_s, left_s, right_s, picks, sizes = input_arrays
    mask = live_mask(sizes)
    live = wave_s * mask
    first = (apply_section(left_s, live, picks, right_s) * mask.astype(jnp.float32)).astype(jnp.bfloat16)
    first_f = first.astype(jnp.float32)
    squares = jnp.sum(first_f * first_f)
    count = jnp.sum((sizes * sizes).astype(jnp.float32))
    scale = lax.rsqrt(squares / count + 1e-06)
    trial_vector = (first_f * scale).astype(jnp.bfloat16)
    left_vector = jnp.einsum('ktab,kbc->ktac', left_s.astype(jnp.float32), trial_vector.astype(jnp.float32)).astype(jnp.bfloat16)
    terms = jnp.einsum('kba,ktbc->ktac', trial_vector.astype(jnp.float32), left_vector.astype(jnp.float32))
    grouped = terms.reshape(NB // BLK_DEV, BLK_DEV, W, SB, SB).sum(axis=1).astype(jnp.bfloat16)
    grouped = lax.optimization_barrier(grouped)
    total = grouped.astype(jnp.float32).sum(axis=0)
    factor = 1.0 / (SB * math.sqrt(NB))
    edge = (total * factor).astype(jnp.bfloat16)
    return (first, trial_vector, edge)

def phase_two(input_arrays):
    trial_vector, left_s, right_s, picks, sizes, incoming = input_arrays
    mask = live_mask(sizes)
    left_two = (left_s.astype(jnp.float32) + incoming[None].astype(jnp.float32)).astype(jnp.bfloat16)
    second_apply = apply_section(left_two, trial_vector, picks, right_s) * mask.astype(jnp.float32)
    return second_apply.astype(jnp.bfloat16)

def reference(wave, left_block_environment, right_block_environment, source_block, sector_size):
    first, trial_vector, edge = lax.map(phase_one, (wave, left_block_environment, right_block_environment, source_block, sector_size))
    incoming = jnp.concatenate([jnp.zeros_like(edge[:1]), edge[:-1]], axis=0)
    second_apply = lax.map(phase_two, (trial_vector, left_block_environment, right_block_environment, source_block, sector_size, incoming))
    return (first, second_apply)
```

```python
import functools
import math

import jax
import jax.numpy as jnp
from jax import lax
from jax.experimental import pallas as pl
from jax.experimental.pallas import tpu as pltpu
from jax.sharding import PartitionSpec as P

MESH = pl.DeviceIdType.MESH
F32 = jnp.float32
BF16 = jnp.bfloat16


def dot(a, b):
    return jnp.dot(a, b, preferred_element_type=F32)


def copies_between(nb, per):
    nx = nb // 2
    return 2 * (2 * nx - 1) + (nb - 1) + nx * per + (nx - 1) * per + per + per * (2 * nx - 1)


def kernel(
    nsec, nb, picks, sizes, wave_h, left_h, right_h, out1_h, out2_h,
    wave_v, left, right, pool, fpool, inner, psend, precv, mine, rsend, rrecv, edge, inc, meta, acc,
    stage, lsem, ssem, rsem,
):
    width = wave_h.shape[-1]
    channels = left_h.shape[0]
    nx = nb // 2
    per = channels // nb
    sec = lax.axis_index("sec")
    me = lax.axis_index("blk")
    chip = me // 2
    core = me % 2
    sib = chip * 2 + 1 - core

    load_wave = pltpu.make_async_copy(wave_h, wave_v, lsem.at[0])
    load_left = pltpu.make_async_copy(left_h, left, lsem.at[1])
    load_right = pltpu.make_async_copy(right_h, right, lsem.at[2])
    load_wave.start()
    load_left.start()
    load_right.start()

    barrier = pltpu.get_barrier_semaphore()
    for o in range(1, nb):
        pl.semaphore_signal(barrier, inc=1, device_id={"blk": (me + o) % nb}, device_id_type=MESH)

    @pl.when(sec > 0)
    def _():
        pl.semaphore_signal(barrier, inc=1, device_id={"sec": sec - 1}, device_id_type=MESH)

    @pl.when(sec < nsec - 1)
    def _():
        pl.semaphore_signal(barrier, inc=1, device_id={"sec": sec + 1}, device_id_type=MESH)

    at = {}
    sent = []

    def remote(key, src, dst, **device):
        k = at.setdefault(key, len(at))
        return pltpu.make_async_remote_copy(
            src_ref=src, dst_ref=dst, send_sem=ssem.at[k], recv_sem=rsem.at[k],
            device_id=device, device_id_type=MESH,
        )

    def send(key, src, dst, **device):
        copy = remote(key, src, dst, **device)
        copy.start()
        sent.append(copy)

    def arrived(key, ref):
        remote(key, ref, ref, blk=sib).wait_recv()

    def same_core(o):
        return ((chip + o) % nx) * 2 + core

    def share(name, ref):
        for o in range(1, nx):
            send((name, "x", o), ref.at[me], ref.at[me], blk=same_core(o))
        send((name, "c", 0), ref.at[me], ref.at[me], blk=sib)

    def pass_on(name, ref):
        for o in range(1, nx):
            block = ref.at[same_core(nx - o)]
            arrived((name, "x", o), block)
            send((name, "c", o), block, block, blk=sib)

    def take(name, ref):
        for o in range(nx):
            arrived((name, "c", o), ref.at[((chip + nx - o) % nx) * 2 + 1 - core])

    size = sizes[0]
    live_at = (lax.broadcasted_iota(jnp.int32, (width, width), 0) < size) & (
        lax.broadcasted_iota(jnp.int32, (width, width), 1) < size
    )
    load_wave.wait()
    pool[me] = jnp.where(live_at, wave_v[...].astype(F32), 0.0).astype(BF16)
    pl.semaphore_wait(
        barrier, nb - 1 + (sec > 0).astype(jnp.int32) + (sec < nsec - 1).astype(jnp.int32)
    )
    share("live", pool)
    load_left.wait()
    load_right.wait()
    pass_on("live", pool)
    take("live", pool)

    for t in range(channels):
        inner[:, t * width:(t + 1) * width] = dot(left[t], pool[picks[t]]).astype(BF16)
    total = dot(inner[...], right[...].reshape(channels * width, width))
    first = jnp.where(live_at, total, 0.0).astype(BF16)
    fpool[me] = first
    share("first", fpool)
    store_first = pltpu.make_async_copy(fpool.at[me], out1_h, lsem.at[3])
    store_first.start()

    first_f = fpool[me].astype(F32)
    first_t = jnp.transpose(first_f).astype(BF16)

    rounds = [(o, j) for o in list(range(1, nx)) + [0] for j in range(per)]

    def combine(r):
        o, j = rounds[r]
        arrived(("part", r), precv.at[r])
        both = mine[r].astype(F32) + precv[r].astype(F32)
        if o == 0:
            acc_at = j
            edge[acc_at] = both.astype(BF16)
        else:
            slot = (o - 1) * per + j
            rsend[slot] = both.astype(BF16)
            send(("rs", o, j), rsend.at[slot], rrecv.at[slot], blk=same_core(o))

    for r, (o, j) in enumerate(rounds):
        q = (chip + o) % nx
        theirs = (q * 2 + 1 - core) * per + j
        own = (q * 2 + core) * per + j
        lv = dot(left[theirs], fpool[me]).astype(BF16)
        psend[r] = dot(first_t, lv).astype(BF16)
        send(("part", r), psend.at[r], precv.at[r], blk=sib)
        lv = dot(left[own], fpool[me]).astype(BF16)
        mine[r] = dot(first_t, lv).astype(BF16)
        if r == 0:
            squares = jnp.sum((first_f * first_f).reshape(width // 8, 8, width), axis=0)
            fold = squares[:, :128]
            for c in range(128, width, 128):
                fold = fold + squares[:, c:c + 128]
            meta[me, :8] = fold
            meta[me, 8:] = jnp.full((8, 128), (size * size).astype(F32), F32)
            for p in range(1, nb):
                send(("meta", p), meta.at[me], meta.at[me], blk=(me + p) % nb)
        if r >= 1:
            combine(r - 1)
    combine(len(rounds) - 1)

    pass_on("first", fpool)
    for p in range(1, nb):
        arrived(("meta", p), meta.at[(me + nb - p) % nb])
    totals = jnp.sum(meta[...], axis=0)
    square_sum = jnp.sum(totals[:8], keepdims=True)
    count = jnp.sum(totals[8:], keepdims=True) * (1.0 / 1024)
    scale = lax.rsqrt(square_sum / count + 1e-06)
    factor = scale * scale * (1.0 / (width * math.sqrt(nb)))
    store_first.wait()
    take("first", fpool)

    later = []

    def up(j):
        result = edge[j].astype(F32)
        for o in range(1, nx):
            slot = (o - 1) * per + j
            arrived(("rs", o, j), rrecv.at[slot])
            result = result + rrecv[slot].astype(F32)
        edge[j] = (result * factor).astype(BF16)
        copy = remote(("up", j), edge.at[j], inc.at[me * per + j], sec=sec + 1)
        later.append(copy)

        @pl.when(sec < nsec - 1)
        def _():
            copy.start()

    inner_sends = []

    def spread(j):
        t = me * per + j
        block = inc.at[t]
        outs = [remote(("inc", j, "x", o), block, block, blk=same_core(o)) for o in range(1, nx)]
        outs.append(remote(("inc", j, "c", 0), block, block, blk=sib))
        inner_sends.extend(outs)

        @pl.when(sec > 0)
        def _():
            arrived(("up", j), block)
            for copy in outs:
                copy.start()

    def hand_on(j):
        pairs = []
        for o in range(1, nx):
            block = inc.at[same_core(nx - o) * per + j]
            pairs.append((o, block, remote(("inc", j, "c", o), block, block, blk=sib)))
        inner_sends.extend(copy for _, _, copy in pairs)

        @pl.when(sec > 0)
        def _():
            for o, block, copy in pairs:
                arrived(("inc", j, "x", o), block)
                copy.start()

    def second(j):
        @pl.when(sec > 0)
        def _():
            for o in range(nx):
                arrived(("inc", j, "c", o), inc.at[(((chip + nx - o) % nx) * 2 + 1 - core) * per + j])

        result = acc[...] if j else None
        for d in range(nb):
            t = d * per + j
            left_two = (left[t].astype(F32) + inc[t].astype(F32)).astype(BF16)
            step = dot(dot(left_two, fpool[picks[t]]).astype(BF16), right[t])
            result = step if result is None else result + step
        acc[...] = result

    @pl.when(sec == 0)
    def _():
        inc[...] = jnp.zeros_like(inc)

    for tick in range(per + 4):
        if tick < per:
            up(tick)
        if 1 <= tick < per + 1:
            spread(tick - 1)
        if 2 <= tick < per + 2:
            hand_on(tick - 2)
        if 3 <= tick < per + 3:
            second(tick - 3)

    stage[...] = jnp.where(live_at, acc[...] * scale, 0.0).astype(BF16)
    store_second = pltpu.make_async_copy(stage, out2_h, lsem.at[4])
    store_second.start()

    for copy in sent:
        copy.wait_send()

    @pl.when(sec < nsec - 1)
    def _():
        for copy in later:
            copy.wait_send()

    @pl.when(sec > 0)
    def _():
        for copy in inner_sends:
            copy.wait_send()

    store_second.wait()


def shards(nsec, nb, wave, left, right, picks, sizes):
    width = wave.shape[-1]
    channels = left.shape[2]
    nx = nb // 2
    per = channels // nb
    block = (width, width)
    copies = copies_between(nb, per)
    vmem = lambda *lead: pltpu.VMEM((*lead, *block), BF16)
    anywhere = pl.BlockSpec(memory_space=pl.ANY)
    smem = pl.BlockSpec(memory_space=pltpu.SMEM)
    out = jax.ShapeDtypeStruct(block, BF16)
    first, second = pl.pallas_call(
        functools.partial(kernel, nsec, nb),
        out_shape=(out, out),
        in_specs=[smem, smem, anywhere, anywhere, anywhere],
        out_specs=(anywhere, anywhere),
        scratch_shapes=[
            vmem(),
            vmem(channels),
            vmem(channels),
            vmem(nb),
            vmem(nb),
            pltpu.VMEM((width, channels * width), BF16),
            vmem(nx * per),
            vmem(nx * per),
            vmem(nx * per),
            vmem((nx - 1) * per),
            vmem((nx - 1) * per),
            vmem(per),
            vmem(channels),
            pltpu.VMEM((nb, 16, 128), F32),
            pltpu.VMEM(block, F32),
            vmem(),
            pltpu.SemaphoreType.DMA((5,)),
            pltpu.SemaphoreType.DMA((copies,)),
            pltpu.SemaphoreType.DMA((copies,)),
        ],
        compiler_params=pltpu.CompilerParams(
            collective_id=0, has_side_effects=True, vmem_limit_bytes=48 * 2**20
        ),
        cost_estimate=pl.CostEstimate(
            flops=12 * channels * width**3, bytes_accessed=4 * channels * width**2, transcendentals=0
        ),
    )(
        picks.reshape(channels),
        sizes.reshape(1),
        wave.reshape(block),
        left.reshape(channels, *block),
        right.reshape(channels, *block),
    )
    return first[None, None], second[None, None]


def solution(mesh):
    return jax.shard_map(
        functools.partial(shards, mesh.shape["sec"], mesh.shape["blk"]),
        mesh=mesh,
        in_specs=(
            P("sec", "blk", None, None),
            P("sec", "blk", None, None, None),
            P("sec", "blk", None, None, None),
            P("sec", "blk", None),
            P("sec", "blk"),
        ),
        out_specs=(P("sec", "blk", None, None), P("sec", "blk", None, None)),
        check_vma=False,
    )
```

```python
import functools
import math

import jax
import jax.numpy as jnp
from jax import lax
from jax.experimental import pallas as pl
from jax.experimental.pallas import tpu as pltpu
from jax.sharding import PartitionSpec as P

MESH = pl.DeviceIdType.MESH
F32 = jnp.float32
BF16 = jnp.bfloat16


def dot(a, b):
    return jnp.dot(a, b, preferred_element_type=F32)


def copies_between(nb, per):
    nx = nb // 2
    return 2 * (2 * nx - 1) + (nb - 1) + nx * per + (nx - 1) * per + per + per * (2 * nx - 1)


def kernel(
    nsec, nb, picks_h, sizes_h, wave_h, left_h, right_h, out1_h, out2_h,
    picks, sizes, wave_v, left, right, pool, fpool, inner, psend, precv, mine, rsend, rrecv, edge, inc, meta, acc,
    stage, lsem, ssem, rsem,
):
    width = wave_h.shape[-1]
    channels = left_h.shape[0]
    nx = nb // 2
    per = channels // nb
    sec = lax.axis_index("sec")
    me = lax.axis_index("blk")
    chip = me // 2
    core = me % 2
    sib = chip * 2 + 1 - core

    load_wave = pltpu.make_async_copy(wave_h, wave_v, lsem.at[0])
    load_left = pltpu.make_async_copy(left_h, left, lsem.at[1])
    load_right = pltpu.make_async_copy(right_h, right, lsem.at[2])
    load_sizes = pltpu.make_async_copy(sizes_h, sizes, lsem.at[5])
    load_picks = pltpu.make_async_copy(picks_h, picks, lsem.at[6])
    load_wave.start()
    load_sizes.start()
    load_picks.start()
    load_left.start()
    load_right.start()

    barrier = pltpu.get_barrier_semaphore()
    for o in range(1, nb):
        pl.semaphore_signal(barrier, inc=1, device_id={"blk": (me + o) % nb}, device_id_type=MESH)

    @pl.when(sec > 0)
    def _():
        pl.semaphore_signal(barrier, inc=1, device_id={"sec": sec - 1}, device_id_type=MESH)

    @pl.when(sec < nsec - 1)
    def _():
        pl.semaphore_signal(barrier, inc=1, device_id={"sec": sec + 1}, device_id_type=MESH)

    at = {}
    sent = []

    def remote(key, src, dst, **device):
        k = at.setdefault(key, len(at))
        return pltpu.make_async_remote_copy(
            src_ref=src, dst_ref=dst, send_sem=ssem.at[k], recv_sem=rsem.at[k],
            device_id=device, device_id_type=MESH,
        )

    def send(key, src, dst, **device):
        copy = remote(key, src, dst, **device)
        copy.start()
        sent.append(copy)

    def arrived(key, ref):
        remote(key, ref, ref, blk=sib).wait_recv()

    def same_core(o):
        return ((chip + o) % nx) * 2 + core

    def share(name, ref):
        for o in range(1, nx):
            send((name, "x", o), ref.at[me], ref.at[me], blk=same_core(o))
        send((name, "c", 0), ref.at[me], ref.at[me], blk=sib)

    def pass_on(name, ref):
        for o in range(1, nx):
            block = ref.at[same_core(nx - o)]
            arrived((name, "x", o), block)
            send((name, "c", o), block, block, blk=sib)

    def take(name, ref):
        for o in range(nx):
            arrived((name, "c", o), ref.at[((chip + nx - o) % nx) * 2 + 1 - core])

    load_sizes.wait()
    load_picks.wait()
    size = sizes[0, 0]
    live_at = (lax.broadcasted_iota(jnp.int32, (width, width), 0) < size) & (
        lax.broadcasted_iota(jnp.int32, (width, width), 1) < size
    )
    load_wave.wait()
    pool[me] = jnp.where(live_at, wave_v[...].astype(F32), 0.0).astype(BF16)
    pl.semaphore_wait(
        barrier, nb - 1 + (sec > 0).astype(jnp.int32) + (sec < nsec - 1).astype(jnp.int32)
    )
    share("live", pool)
    load_left.wait()
    load_right.wait()
    pass_on("live", pool)
    take("live", pool)

    for t in range(channels):
        inner[:, t * width:(t + 1) * width] = dot(left[t], pool[picks[0, t]]).astype(BF16)
    total = dot(inner[...], right[...].reshape(channels * width, width))
    first = jnp.where(live_at, total, 0.0).astype(BF16)
    fpool[me] = first
    share("first", fpool)
    store_first = pltpu.make_async_copy(fpool.at[me], out1_h, lsem.at[3])
    store_first.start()

    first_f = fpool[me].astype(F32)
    first_t = jnp.transpose(first_f).astype(BF16)

    rounds = [(o, j) for o in list(range(1, nx)) + [0] for j in range(per)]

    def combine(r):
        o, j = rounds[r]
        arrived(("part", r), precv.at[r])
        both = mine[r].astype(F32) + precv[r].astype(F32)
        if o == 0:
            acc_at = j
            edge[acc_at] = both.astype(BF16)
        else:
            slot = (o - 1) * per + j
            rsend[slot] = both.astype(BF16)
            send(("rs", o, j), rsend.at[slot], rrecv.at[slot], blk=same_core(o))

    for r, (o, j) in enumerate(rounds):
        q = (chip + o) % nx
        theirs = (q * 2 + 1 - core) * per + j
        own = (q * 2 + core) * per + j
        lv = dot(left[theirs], fpool[me]).astype(BF16)
        psend[r] = dot(first_t, lv).astype(BF16)
        send(("part", r), psend.at[r], precv.at[r], blk=sib)
        lv = dot(left[own], fpool[me]).astype(BF16)
        mine[r] = dot(first_t, lv).astype(BF16)
        if r == 0:
            squares = jnp.sum((first_f * first_f).reshape(width // 8, 8, width), axis=0)
            fold = squares[:, :128]
            for c in range(128, width, 128):
                fold = fold + squares[:, c:c + 128]
            meta[me, :8] = fold
            meta[me, 8:] = jnp.full((8, 128), (size * size).astype(F32), F32)
            for p in range(1, nb):
                send(("meta", p), meta.at[me], meta.at[me], blk=(me + p) % nb)
        if r >= 1:
            combine(r - 1)
    combine(len(rounds) - 1)

    pass_on("first", fpool)
    for p in range(1, nb):
        arrived(("meta", p), meta.at[(me + nb - p) % nb])
    totals = jnp.sum(meta[...], axis=0)
    square_sum = jnp.sum(totals[:8], keepdims=True)
    count = jnp.sum(totals[8:], keepdims=True) * (1.0 / 1024)
    scale = lax.rsqrt(square_sum / count + 1e-06)
    factor = scale * scale * (1.0 / (width * math.sqrt(nb)))
    store_first.wait()
    take("first", fpool)

    later = []

    def up(j):
        result = edge[j].astype(F32)
        for o in range(1, nx):
            slot = (o - 1) * per + j
            arrived(("rs", o, j), rrecv.at[slot])
            result = result + rrecv[slot].astype(F32)
        edge[j] = (result * factor).astype(BF16)
        copy = remote(("up", j), edge.at[j], inc.at[me * per + j], sec=sec + 1)
        later.append(copy)

        @pl.when(sec < nsec - 1)
        def _():
            copy.start()

    inner_sends = []

    def spread(j):
        t = me * per + j
        block = inc.at[t]
        outs = [remote(("inc", j, "x", o), block, block, blk=same_core(o)) for o in range(1, nx)]
        outs.append(remote(("inc", j, "c", 0), block, block, blk=sib))
        inner_sends.extend(outs)

        @pl.when(sec > 0)
        def _():
            arrived(("up", j), block)
            for copy in outs:
                copy.start()

    def hand_on(j):
        pairs = []
        for o in range(1, nx):
            block = inc.at[same_core(nx - o) * per + j]
            pairs.append((o, block, remote(("inc", j, "c", o), block, block, blk=sib)))
        inner_sends.extend(copy for _, _, copy in pairs)

        @pl.when(sec > 0)
        def _():
            for o, block, copy in pairs:
                arrived(("inc", j, "x", o), block)
                copy.start()

    def second(j):
        @pl.when(sec > 0)
        def _():
            for o in range(nx):
                arrived(("inc", j, "c", o), inc.at[(((chip + nx - o) % nx) * 2 + 1 - core) * per + j])

        result = acc[...] if j else None
        for d in range(nb):
            t = d * per + j
            left_two = (left[t].astype(F32) + inc[t].astype(F32)).astype(BF16)
            step = dot(dot(left_two, fpool[picks[0, t]]).astype(BF16), right[t])
            result = step if result is None else result + step
        acc[...] = result

    @pl.when(sec == 0)
    def _():
        inc[...] = jnp.zeros_like(inc)

    for tick in range(per + 4):
        if tick < per:
            up(tick)
        if 1 <= tick < per + 1:
            spread(tick - 1)
        if 2 <= tick < per + 2:
            hand_on(tick - 2)
        if 3 <= tick < per + 3:
            second(tick - 3)

    stage[...] = jnp.where(live_at, acc[...] * scale, 0.0).astype(BF16)
    store_second = pltpu.make_async_copy(stage, out2_h, lsem.at[4])
    store_second.start()

    for copy in sent:
        copy.wait_send()

    @pl.when(sec < nsec - 1)
    def _():
        for copy in later:
            copy.wait_send()

    @pl.when(sec > 0)
    def _():
        for copy in inner_sends:
            copy.wait_send()

    store_second.wait()


def shards(nsec, nb, wave, left, right, picks, sizes):
    width = wave.shape[-1]
    channels = left.shape[2]
    nx = nb // 2
    per = channels // nb
    block = (width, width)
    copies = copies_between(nb, per)
    vmem = lambda *lead: pltpu.VMEM((*lead, *block), BF16)
    anywhere = pl.BlockSpec(memory_space=pltpu.HBM)
    out = jax.ShapeDtypeStruct(block, BF16)
    first, second = pl.pallas_call(
        functools.partial(kernel, nsec, nb),
        out_shape=(out, out),
        in_specs=[anywhere] * 5,
        out_specs=(anywhere, anywhere),
        scratch_shapes=[
            pltpu.SMEM((1, channels), jnp.int32),
            pltpu.SMEM((1, 1), jnp.int32),
            vmem(),
            vmem(channels),
            vmem(channels),
            vmem(nb),
            vmem(nb),
            pltpu.VMEM((width, channels * width), BF16),
            vmem(nx * per),
            vmem(nx * per),
            vmem(nx * per),
            vmem((nx - 1) * per),
            vmem((nx - 1) * per),
            vmem(per),
            vmem(channels),
            pltpu.VMEM((nb, 16, 128), F32),
            pltpu.VMEM(block, F32),
            vmem(),
            pltpu.SemaphoreType.DMA((7,)),
            pltpu.SemaphoreType.DMA((copies,)),
            pltpu.SemaphoreType.DMA((copies,)),
        ],
        compiler_params=pltpu.CompilerParams(
            collective_id=0, has_side_effects=True, vmem_limit_bytes=62 * 2**20
        ),
        cost_estimate=pl.CostEstimate(
            flops=12 * channels * width**3, bytes_accessed=4 * channels * width**2, transcendentals=0
        ),
    )(
        picks.reshape(1, channels),
        sizes.reshape(1, 1),
        wave.reshape(block),
        left.reshape(channels, *block),
        right.reshape(channels, *block),
    )
    return first[None, None], second[None, None]


def solution(mesh):
    return jax.shard_map(
        functools.partial(shards, mesh.shape["sec"], mesh.shape["blk"]),
        mesh=mesh,
        in_specs=(
            P("sec", "blk", None, None),
            P("sec", "blk", None, None, None),
            P("sec", "blk", None, None, None),
            P("sec", "blk", None),
            P("sec", "blk"),
        ),
        out_specs=(P("sec", "blk", None, None), P("sec", "blk", None, None)),
        check_vma=False,
    )
```

```python
import functools
import math

import jax
import jax.numpy as jnp
from jax import lax
from jax.experimental import pallas as pl
from jax.experimental.pallas import tpu as pltpu
from jax.sharding import PartitionSpec as P

MESH = pl.DeviceIdType.MESH
F32 = jnp.float32
BF16 = jnp.bfloat16


def dot(a, b):
    return jnp.dot(a, b, preferred_element_type=F32)


def copies_between(nb, per):
    nx = nb // 2
    return 2 * (2 * nx - 1) + (nb - 1) + nx * per + (nx - 1) * per + per + per * (2 * nx - 1)


def kernel(
    nsec, nb, picks_h, sizes_h, wave_h, left_h, right_h, out1, out2,
    picks, sizes, wave_v, left, right, pool, fpool, inner, psend, precv, mine, rsend, rrecv, edge, inc, meta, acc,
    lsem, ssem, rsem,
):
    width = wave_h.shape[-1]
    channels = left_h.shape[0]
    nx = nb // 2
    per = channels // nb
    sec = lax.axis_index("sec")
    me = lax.axis_index("blk")
    chip = me // 2
    core = me % 2
    sib = chip * 2 + 1 - core

    load_wave = pltpu.make_async_copy(wave_h, wave_v, lsem.at[0])
    load_left = pltpu.make_async_copy(left_h, left, lsem.at[1])
    load_right = pltpu.make_async_copy(right_h, right, lsem.at[2])
    load_sizes = pltpu.make_async_copy(sizes_h, sizes, lsem.at[3])
    load_picks = pltpu.make_async_copy(picks_h, picks, lsem.at[4])
    load_wave.start()
    load_sizes.start()
    load_picks.start()
    load_left.start()
    load_right.start()

    barrier = pltpu.get_barrier_semaphore()
    for o in range(1, nb):
        pl.semaphore_signal(barrier, inc=1, device_id={"blk": (me + o) % nb}, device_id_type=MESH)

    @pl.when(sec > 0)
    def _():
        pl.semaphore_signal(barrier, inc=1, device_id={"sec": sec - 1}, device_id_type=MESH)

    @pl.when(sec < nsec - 1)
    def _():
        pl.semaphore_signal(barrier, inc=1, device_id={"sec": sec + 1}, device_id_type=MESH)

    at = {}
    sent = []

    def remote(key, src, dst, **device):
        k = at.setdefault(key, len(at))
        return pltpu.make_async_remote_copy(
            src_ref=src, dst_ref=dst, send_sem=ssem.at[k], recv_sem=rsem.at[k],
            device_id=device, device_id_type=MESH,
        )

    def send(key, src, dst, **device):
        copy = remote(key, src, dst, **device)
        copy.start()
        sent.append(copy)

    def arrived(key, ref):
        remote(key, ref, ref, blk=sib).wait_recv()

    def same_core(o):
        return ((chip + o) % nx) * 2 + core

    def share(name, ref):
        for o in range(1, nx):
            send((name, "x", o), ref.at[me], ref.at[me], blk=same_core(o))
        send((name, "c", 0), ref.at[me], ref.at[me], blk=sib)

    def pass_on(name, ref):
        for o in range(1, nx):
            block = ref.at[same_core(nx - o)]
            arrived((name, "x", o), block)
            send((name, "c", o), block, block, blk=sib)

    def take(name, ref):
        for o in range(nx):
            arrived((name, "c", o), ref.at[((chip + nx - o) % nx) * 2 + 1 - core])

    load_sizes.wait()
    load_picks.wait()
    size = sizes[0, 0]
    live_at = (lax.broadcasted_iota(jnp.int32, (width, width), 0) < size) & (
        lax.broadcasted_iota(jnp.int32, (width, width), 1) < size
    )
    load_wave.wait()
    pool[me] = jnp.where(live_at, wave_v[...].astype(F32), 0.0).astype(BF16)
    pl.semaphore_wait(
        barrier, nb - 1 + (sec > 0).astype(jnp.int32) + (sec < nsec - 1).astype(jnp.int32)
    )
    share("live", pool)
    load_left.wait()
    load_right.wait()
    pass_on("live", pool)
    take("live", pool)

    for t in range(channels):
        inner[:, t * width:(t + 1) * width] = dot(left[t], pool[picks[0, t]]).astype(BF16)
    total = dot(inner[...], right[...].reshape(channels * width, width))
    first = jnp.where(live_at, total, 0.0).astype(BF16)
    fpool[me] = first
    share("first", fpool)
    out1[...] = first

    first_f = fpool[me].astype(F32)
    first_t = jnp.transpose(first_f).astype(BF16)

    rounds = [(o, j) for o in list(range(1, nx)) + [0] for j in range(per)]

    def combine(r):
        o, j = rounds[r]
        arrived(("part", r), precv.at[r])
        both = mine[r].astype(F32) + precv[r].astype(F32)
        if o == 0:
            acc_at = j
            edge[acc_at] = both.astype(BF16)
        else:
            slot = (o - 1) * per + j
            rsend[slot] = both.astype(BF16)
            send(("rs", o, j), rsend.at[slot], rrecv.at[slot], blk=same_core(o))

    for r, (o, j) in enumerate(rounds):
        q = (chip + o) % nx
        theirs = (q * 2 + 1 - core) * per + j
        own = (q * 2 + core) * per + j
        lv = dot(left[theirs], fpool[me]).astype(BF16)
        psend[r] = dot(first_t, lv).astype(BF16)
        send(("part", r), psend.at[r], precv.at[r], blk=sib)
        lv = dot(left[own], fpool[me]).astype(BF16)
        mine[r] = dot(first_t, lv).astype(BF16)
        if r == 0:
            squares = jnp.sum((first_f * first_f).reshape(width // 8, 8, width), axis=0)
            fold = squares[:, :128]
            for c in range(128, width, 128):
                fold = fold + squares[:, c:c + 128]
            meta[me, :8] = fold
            meta[me, 8:] = jnp.full((8, 128), (size * size).astype(F32), F32)
            for p in range(1, nb):
                send(("meta", p), meta.at[me], meta.at[me], blk=(me + p) % nb)
        if r >= 1:
            combine(r - 1)
    combine(len(rounds) - 1)

    pass_on("first", fpool)
    for p in range(1, nb):
        arrived(("meta", p), meta.at[(me + nb - p) % nb])
    totals = jnp.sum(meta[...], axis=0)
    square_sum = jnp.sum(totals[:8], keepdims=True)
    count = jnp.sum(totals[8:], keepdims=True) * (1.0 / 1024)
    scale = lax.rsqrt(square_sum / count + 1e-06)
    factor = scale * scale * (1.0 / (width * math.sqrt(nb)))
    take("first", fpool)

    later = []

    def up(j):
        result = edge[j].astype(F32)
        for o in range(1, nx):
            slot = (o - 1) * per + j
            arrived(("rs", o, j), rrecv.at[slot])
            result = result + rrecv[slot].astype(F32)
        edge[j] = (result * factor).astype(BF16)
        copy = remote(("up", j), edge.at[j], inc.at[me * per + j], sec=sec + 1)
        later.append(copy)

        @pl.when(sec < nsec - 1)
        def _():
            copy.start()

    inner_sends = []

    def spread(j):
        t = me * per + j
        block = inc.at[t]
        outs = [remote(("inc", j, "x", o), block, block, blk=same_core(o)) for o in range(1, nx)]
        outs.append(remote(("inc", j, "c", 0), block, block, blk=sib))
        inner_sends.extend(outs)

        @pl.when(sec > 0)
        def _():
            arrived(("up", j), block)
            for copy in outs:
                copy.start()

    def hand_on(j):
        pairs = []
        for o in range(1, nx):
            block = inc.at[same_core(nx - o) * per + j]
            pairs.append((o, block, remote(("inc", j, "c", o), block, block, blk=sib)))
        inner_sends.extend(copy for _, _, copy in pairs)

        @pl.when(sec > 0)
        def _():
            for o, block, copy in pairs:
                arrived(("inc", j, "x", o), block)
                copy.start()

    def second(j):
        @pl.when(sec > 0)
        def _():
            for o in range(nx):
                arrived(("inc", j, "c", o), inc.at[(((chip + nx - o) % nx) * 2 + 1 - core) * per + j])

        result = acc[...] if j else None
        for d in range(nb):
            t = d * per + j
            left_two = (left[t].astype(F32) + inc[t].astype(F32)).astype(BF16)
            step = dot(dot(left_two, fpool[picks[0, t]]).astype(BF16), right[t])
            result = step if result is None else result + step
        acc[...] = result

    @pl.when(sec == 0)
    def _():
        inc[...] = jnp.zeros_like(inc)

    for tick in range(per + 4):
        if tick < per:
            up(tick)
        if 1 <= tick < per + 1:
            spread(tick - 1)
        if 2 <= tick < per + 2:
            hand_on(tick - 2)
        if 3 <= tick < per + 3:
            second(tick - 3)

    out2[...] = jnp.where(live_at, acc[...] * scale, 0.0).astype(BF16)

    for copy in sent:
        copy.wait_send()

    @pl.when(sec < nsec - 1)
    def _():
        for copy in later:
            copy.wait_send()

    @pl.when(sec > 0)
    def _():
        for copy in inner_sends:
            copy.wait_send()


def write_out(first, second, first_h, second_h, sem):
    copies = [
        pltpu.make_async_copy(first, first_h, sem.at[0]),
        pltpu.make_async_copy(second, second_h, sem.at[1]),
    ]
    for copy in copies:
        copy.start()
    for copy in copies:
        copy.wait()


def shards(nsec, nb, wave, left, right, picks, sizes):
    width = wave.shape[-1]
    channels = left.shape[2]
    nx = nb // 2
    per = channels // nb
    block = (width, width)
    copies = copies_between(nb, per)
    vmem = lambda *lead: pltpu.VMEM((*lead, *block), BF16)
    anywhere = pl.BlockSpec(memory_space=pltpu.HBM)
    out = pltpu.VMEM(block, BF16)
    first, second = pl.pallas_call(
        functools.partial(kernel, nsec, nb),
        out_shape=(out, out),
        in_specs=[anywhere] * 5,
        out_specs=(pl.BlockSpec(memory_space=pltpu.VMEM),) * 2,
        scratch_shapes=[
            pltpu.SMEM((1, channels), jnp.int32),
            pltpu.SMEM((1, 1), jnp.int32),
            vmem(),
            vmem(channels),
            vmem(channels),
            vmem(nb),
            vmem(nb),
            pltpu.VMEM((width, channels * width), BF16),
            vmem(nx * per),
            vmem(nx * per),
            vmem(nx * per),
            vmem((nx - 1) * per),
            vmem((nx - 1) * per),
            vmem(per),
            vmem(channels),
            pltpu.VMEM((nb, 16, 128), F32),
            pltpu.VMEM(block, F32),
            pltpu.SemaphoreType.DMA((5,)),
            pltpu.SemaphoreType.DMA((copies,)),
            pltpu.SemaphoreType.DMA((copies,)),
        ],
        compiler_params=pltpu.CompilerParams(
            collective_id=0, has_side_effects=True, vmem_limit_bytes=62 * 2**20
        ),
        cost_estimate=pl.CostEstimate(
            flops=12 * channels * width**3, bytes_accessed=4 * channels * width**2, transcendentals=0
        ),
    )(
        picks.reshape(1, channels),
        sizes.reshape(1, 1),
        wave.reshape(block),
        left.reshape(channels, *block),
        right.reshape(channels, *block),
    )
    result = jax.ShapeDtypeStruct(block, BF16)
    first, second = pl.pallas_call(
        write_out,
        out_shape=(result, result),
        in_specs=[pl.BlockSpec(memory_space=pltpu.VMEM)] * 2,
        out_specs=(pl.BlockSpec(memory_space=pl.ANY),) * 2,
        scratch_shapes=[pltpu.SemaphoreType.DMA((2,))],
        compiler_params=pltpu.CompilerParams(has_side_effects=True),
    )(*(pltpu.with_memory_space_constraint(x, pltpu.VMEM) for x in (first, second)))
    return first[None, None], second[None, None]


def solution(mesh):
    return jax.shard_map(
        functools.partial(shards, mesh.shape["sec"], mesh.shape["blk"]),
        mesh=mesh,
        in_specs=(
            P("sec", "blk", None, None),
            P("sec", "blk", None, None, None),
            P("sec", "blk", None, None, None),
            P("sec", "blk", None),
            P("sec", "blk"),
        ),
        out_specs=(P("sec", "blk", None, None), P("sec", "blk", None, None)),
        check_vma=False,
    )
```

```python
import functools
import math

import jax
import jax.numpy as jnp
from jax import lax
from jax.experimental import pallas as pl
from jax.experimental.pallas import tpu as pltpu
from jax.sharding import PartitionSpec as P

MESH = pl.DeviceIdType.MESH
F32 = jnp.float32
BF16 = jnp.bfloat16


def dot(a, b):
    return jnp.dot(a, b, preferred_element_type=F32)


def copies_between(nb, per):
    nx = nb // 2
    return (
        2 * (2 * nx - 1) + (nb - 1) + nx * per + (nx - 1) * per + per + per * (2 * nx - 1)
        + 2 * (nx - 1) * ahead(nb, per)
    )


def ahead(nb, per):
    return 1 if per > 1 else 0


def kernel(
    nsec, nb, picks_h, sizes_h, wave_h, left_h, right_h, out1, out2,
    picks, sizes, wave_v, left, right, pool, fpool, inner, psend, precv, mine, rsend, rrecv, edge, inc, meta, acc, lpre, tpre,
    lsem, ssem, rsem,
):
    width = wave_h.shape[-1]
    channels = left_h.shape[0]
    nx = nb // 2
    per = channels // nb
    pre = ahead(nb, per)
    sec = lax.axis_index("sec")
    me = lax.axis_index("blk")
    chip = me // 2
    core = me % 2
    sib = chip * 2 + 1 - core

    load_wave = pltpu.make_async_copy(wave_h, wave_v, lsem.at[0])
    load_left = pltpu.make_async_copy(left_h, left, lsem.at[1])
    load_right = pltpu.make_async_copy(right_h, right, lsem.at[2])
    load_sizes = pltpu.make_async_copy(sizes_h, sizes, lsem.at[3])
    load_picks = pltpu.make_async_copy(picks_h, picks, lsem.at[4])
    load_wave.start()
    load_sizes.start()
    load_picks.start()
    load_left.start()
    load_right.start()

    barrier = pltpu.get_barrier_semaphore()
    for o in range(1, nb):
        pl.semaphore_signal(barrier, inc=1, device_id={"blk": (me + o) % nb}, device_id_type=MESH)

    @pl.when(sec > 0)
    def _():
        pl.semaphore_signal(barrier, inc=1, device_id={"sec": sec - 1}, device_id_type=MESH)

    @pl.when(sec < nsec - 1)
    def _():
        pl.semaphore_signal(barrier, inc=1, device_id={"sec": sec + 1}, device_id_type=MESH)

    at = {}
    sent = []

    def remote(key, src, dst, **device):
        k = at.setdefault(key, len(at))
        return pltpu.make_async_remote_copy(
            src_ref=src, dst_ref=dst, send_sem=ssem.at[k], recv_sem=rsem.at[k],
            device_id=device, device_id_type=MESH,
        )

    def send(key, src, dst, **device):
        copy = remote(key, src, dst, **device)
        copy.start()
        sent.append(copy)

    def arrived(key, ref):
        remote(key, ref, ref, blk=sib).wait_recv()

    def same_core(o):
        return ((chip + o) % nx) * 2 + core

    def share(name, ref):
        for o in range(1, nx):
            send((name, "x", o), ref.at[me], ref.at[me], blk=same_core(o))
        send((name, "c", 0), ref.at[me], ref.at[me], blk=sib)

    def pass_on(name, ref):
        for o in range(1, nx):
            block = ref.at[same_core(nx - o)]
            arrived((name, "x", o), block)
            send((name, "c", o), block, block, blk=sib)

    def take(name, ref):
        for o in range(nx):
            arrived((name, "c", o), ref.at[((chip + nx - o) % nx) * 2 + 1 - core])

    load_sizes.wait()
    load_picks.wait()
    size = sizes[0, 0]
    live_at = (lax.broadcasted_iota(jnp.int32, (width, width), 0) < size) & (
        lax.broadcasted_iota(jnp.int32, (width, width), 1) < size
    )
    load_wave.wait()
    pool[me] = jnp.where(live_at, wave_v[...].astype(F32), 0.0).astype(BF16)
    pl.semaphore_wait(
        barrier, nb - 1 + (sec > 0).astype(jnp.int32) + (sec < nsec - 1).astype(jnp.int32)
    )
    share("live", pool)
    load_left.wait()
    for o in range(1, nx):
        for j in range(pre):
            for c in range(2):
                channel = (((chip + o) % nx) * 2 + c) * per + j
                send(
                    ("left", o, j, c), left.at[channel], lpre.at[((o - 1) * pre + j) * 2 + c],
                    blk=same_core(o),
                )
    pass_on("live", pool)
    load_right.wait()
    take("live", pool)

    for t in range(channels):
        inner[:, t * width:(t + 1) * width] = dot(left[t], pool[picks[0, t]]).astype(BF16)
    total = dot(inner[...], right[...].reshape(channels * width, width))
    first = jnp.where(live_at, total, 0.0).astype(BF16)
    fpool[me] = first
    share("first", fpool)
    out1[...] = first

    first_f = fpool[me].astype(F32)
    first_t = jnp.transpose(first_f).astype(BF16)

    rounds = [(o, j) for o in list(range(1, nx)) + [0] for j in range(pre, per)]
    rounds += [(0, j) for j in range(pre)]

    def partial(o, j, c):
        channel = (((chip + o) % nx) * 2 + c) * per + j
        term = dot(first_t, dot(left[channel], fpool[me]).astype(BF16))
        if j < pre:
            for p in range(1, nx):
                lv = dot(lpre[((p - 1) * pre + j) * 2 + c], fpool[same_core(nx - p)]).astype(BF16)
                term = term + dot(tpre[p - 1], lv)
        return term.astype(BF16)

    def combine(r):
        o, j = rounds[r]
        arrived(("part", r), precv.at[r])
        both = mine[r].astype(F32) + precv[r].astype(F32)
        if o == 0:
            acc_at = j
            edge[acc_at] = both.astype(BF16)
        else:
            slot = (o - 1) * per + j
            rsend[slot] = both.astype(BF16)
            send(("rs", o, j), rsend.at[slot], rrecv.at[slot], blk=same_core(o))

    for r, (o, j) in enumerate(rounds):
        if j < pre and j == 0:
            pass_on("first", fpool)
            for p in range(1, nx):
                tpre[p - 1] = jnp.transpose(fpool[same_core(nx - p)].astype(F32)).astype(BF16)
                for i in range(pre):
                    for c in range(2):
                        slot = ((p - 1) * pre + i) * 2 + c
                        arrived(("left", p, i, c), lpre.at[slot])
        psend[r] = partial(o, j, 1 - core)
        send(("part", r), psend.at[r], precv.at[r], blk=sib)
        mine[r] = partial(o, j, core)
        if r == 0:
            squares = jnp.sum((first_f * first_f).reshape(width // 8, 8, width), axis=0)
            fold = squares[:, :128]
            for c in range(128, width, 128):
                fold = fold + squares[:, c:c + 128]
            meta[me, :8] = fold
            meta[me, 8:] = jnp.full((8, 128), (size * size).astype(F32), F32)
            for p in range(1, nb):
                send(("meta", p), meta.at[me], meta.at[me], blk=(me + p) % nb)
        if r >= 1:
            combine(r - 1)
    combine(len(rounds) - 1)

    if not pre:
        pass_on("first", fpool)
    for p in range(1, nb):
        arrived(("meta", p), meta.at[(me + nb - p) % nb])
    totals = jnp.sum(meta[...], axis=0)
    square_sum = jnp.sum(totals[:8], keepdims=True)
    count = jnp.sum(totals[8:], keepdims=True) * (1.0 / 1024)
    scale = lax.rsqrt(square_sum / count + 1e-06)
    factor = scale * scale * (1.0 / (width * math.sqrt(nb)))
    take("first", fpool)

    later = []

    def up(j):
        result = edge[j].astype(F32)
        for o in range(1, nx if j >= pre else 1):
            slot = (o - 1) * per + j
            arrived(("rs", o, j), rrecv.at[slot])
            result = result + rrecv[slot].astype(F32)
        edge[j] = (result * factor).astype(BF16)
        copy = remote(("up", j), edge.at[j], inc.at[me * per + j], sec=sec + 1)
        later.append(copy)

        @pl.when(sec < nsec - 1)
        def _():
            copy.start()

    inner_sends = []

    def spread(j):
        t = me * per + j
        block = inc.at[t]
        outs = [remote(("inc", j, "x", o), block, block, blk=same_core(o)) for o in range(1, nx)]
        outs.append(remote(("inc", j, "c", 0), block, block, blk=sib))
        inner_sends.extend(outs)

        @pl.when(sec > 0)
        def _():
            arrived(("up", j), block)
            for copy in outs:
                copy.start()

    def hand_on(j):
        pairs = []
        for o in range(1, nx):
            block = inc.at[same_core(nx - o) * per + j]
            pairs.append((o, block, remote(("inc", j, "c", o), block, block, blk=sib)))
        inner_sends.extend(copy for _, _, copy in pairs)

        @pl.when(sec > 0)
        def _():
            for o, block, copy in pairs:
                arrived(("inc", j, "x", o), block)
                copy.start()

    def second(j):
        @pl.when(sec > 0)
        def _():
            for o in range(nx):
                arrived(("inc", j, "c", o), inc.at[(((chip + nx - o) % nx) * 2 + 1 - core) * per + j])

        result = acc[...] if j else None
        for d in range(nb):
            t = d * per + j
            left_two = (left[t].astype(F32) + inc[t].astype(F32)).astype(BF16)
            step = dot(dot(left_two, fpool[picks[0, t]]).astype(BF16), right[t])
            result = step if result is None else result + step
        acc[...] = result

    @pl.when(sec == 0)
    def _():
        inc[...] = jnp.zeros_like(inc)

    for tick in range(per + 4):
        if tick < per:
            up(tick)
        if 1 <= tick < per + 1:
            spread(tick - 1)
        if 2 <= tick < per + 2:
            hand_on(tick - 2)
        if 3 <= tick < per + 3:
            second(tick - 3)

    out2[...] = jnp.where(live_at, acc[...] * scale, 0.0).astype(BF16)

    for copy in sent:
        copy.wait_send()

    @pl.when(sec < nsec - 1)
    def _():
        for copy in later:
            copy.wait_send()

    @pl.when(sec > 0)
    def _():
        for copy in inner_sends:
            copy.wait_send()


def write_out(first, second, first_h, second_h, sem):
    copies = [
        pltpu.make_async_copy(first, first_h, sem.at[0]),
        pltpu.make_async_copy(second, second_h, sem.at[1]),
    ]
    for copy in copies:
        copy.start()
    for copy in copies:
        copy.wait()


def shards(nsec, nb, wave, left, right, picks, sizes):
    width = wave.shape[-1]
    channels = left.shape[2]
    nx = nb // 2
    per = channels // nb
    block = (width, width)
    copies = copies_between(nb, per)
    pre = ahead(nb, per)
    vmem = lambda *lead: pltpu.VMEM((*lead, *block), BF16)
    anywhere = pl.BlockSpec(memory_space=pltpu.HBM)
    out = pltpu.VMEM(block, BF16)
    first, second = pl.pallas_call(
        functools.partial(kernel, nsec, nb),
        out_shape=(out, out),
        in_specs=[anywhere] * 5,
        out_specs=(pl.BlockSpec(memory_space=pltpu.VMEM),) * 2,
        scratch_shapes=[
            pltpu.SMEM((1, channels), jnp.int32),
            pltpu.SMEM((1, 1), jnp.int32),
            vmem(),
            vmem(channels),
            vmem(channels),
            vmem(nb),
            vmem(nb),
            pltpu.VMEM((width, channels * width), BF16),
            vmem(nx * per),
            vmem(nx * per),
            vmem(nx * per),
            vmem((nx - 1) * per),
            vmem((nx - 1) * per),
            vmem(per),
            vmem(channels),
            pltpu.VMEM((nb, 16, 128), F32),
            pltpu.VMEM(block, F32),
            vmem(max(1, 2 * (nx - 1) * pre)),
            vmem(nx - 1),
            pltpu.SemaphoreType.DMA((5,)),
            pltpu.SemaphoreType.DMA((copies,)),
            pltpu.SemaphoreType.DMA((copies,)),
        ],
        compiler_params=pltpu.CompilerParams(
            collective_id=0, has_side_effects=True, vmem_limit_bytes=62 * 2**20
        ),
        cost_estimate=pl.CostEstimate(
            flops=12 * channels * width**3, bytes_accessed=4 * channels * width**2, transcendentals=0
        ),
    )(
        picks.reshape(1, channels),
        sizes.reshape(1, 1),
        wave.reshape(block),
        left.reshape(channels, *block),
        right.reshape(channels, *block),
    )
    result = jax.ShapeDtypeStruct(block, BF16)
    first, second = pl.pallas_call(
        write_out,
        out_shape=(result, result),
        in_specs=[pl.BlockSpec(memory_space=pltpu.VMEM)] * 2,
        out_specs=(pl.BlockSpec(memory_space=pl.ANY),) * 2,
        scratch_shapes=[pltpu.SemaphoreType.DMA((2,))],
        compiler_params=pltpu.CompilerParams(has_side_effects=True),
    )(*(pltpu.with_memory_space_constraint(x, pltpu.VMEM) for x in (first, second)))
    return first[None, None], second[None, None]


def solution(mesh):
    return jax.shard_map(
        functools.partial(shards, mesh.shape["sec"], mesh.shape["blk"]),
        mesh=mesh,
        in_specs=(
            P("sec", "blk", None, None),
            P("sec", "blk", None, None, None),
            P("sec", "blk", None, None, None),
            P("sec", "blk", None),
            P("sec", "blk"),
        ),
        out_specs=(P("sec", "blk", None, None), P("sec", "blk", None, None)),
        check_vma=False,
    )
```

```python
import functools
import math

import jax
import jax.numpy as jnp
from jax import lax
from jax.experimental import pallas as pl
from jax.experimental.pallas import tpu as pltpu
from jax.sharding import PartitionSpec as P

MESH = pl.DeviceIdType.MESH
F32 = jnp.float32
BF16 = jnp.bfloat16


def dot(a, b):
    return jnp.dot(a, b, preferred_element_type=F32)


def copies_between(nb, per):
    nx = nb // 2
    return (
        2 * (2 * nx - 1) + (nb - 1) + nx * per + (nx - 1) * per + per + per * (2 * nx - 1)
        + 2 * (nx - 1) * ahead(nb, per)
    )


def ahead(nb, per):
    return 1 if per > 1 else 0


def kernel(
    nsec, nb, picks_h, sizes_h, wave_h, left_h, right_h, out1, out2,
    picks, sizes, wave_v, left, right, pool, fpool, inner, psend, precv, mine, rsend, rrecv, edge, inc, meta, acc, lpre, tpre,
    lsem, ssem, rsem,
):
    width = wave_h.shape[-1]
    channels = left_h.shape[0]
    nx = nb // 2
    per = channels // nb
    pre = ahead(nb, per)
    sec = lax.axis_index("sec")
    me = lax.axis_index("blk")
    chip = me // 2
    core = me % 2
    sib = chip * 2 + 1 - core

    load_wave = pltpu.make_async_copy(wave_h, wave_v, lsem.at[0])
    load_left = pltpu.make_async_copy(left_h, left, lsem.at[1])
    load_right = pltpu.make_async_copy(right_h, right, lsem.at[2])
    load_sizes = pltpu.make_async_copy(sizes_h, sizes, lsem.at[3])
    load_picks = pltpu.make_async_copy(picks_h, picks, lsem.at[4])
    load_wave.start()
    load_sizes.start()
    load_picks.start()
    load_left.start()
    load_right.start()

    barrier = pltpu.get_barrier_semaphore()
    for o in range(1, nb):
        pl.semaphore_signal(barrier, inc=1, device_id={"blk": (me + o) % nb}, device_id_type=MESH)

    @pl.when(sec > 0)
    def _():
        pl.semaphore_signal(barrier, inc=1, device_id={"sec": sec - 1}, device_id_type=MESH)

    @pl.when(sec < nsec - 1)
    def _():
        pl.semaphore_signal(barrier, inc=1, device_id={"sec": sec + 1}, device_id_type=MESH)

    at = {}
    sent = []

    def remote(key, src, dst, **device):
        k = at.setdefault(key, len(at))
        return pltpu.make_async_remote_copy(
            src_ref=src, dst_ref=dst, send_sem=ssem.at[k], recv_sem=rsem.at[k],
            device_id=device, device_id_type=MESH,
        )

    def send(key, src, dst, **device):
        copy = remote(key, src, dst, **device)
        copy.start()
        sent.append(copy)

    def arrived(key, ref):
        remote(key, ref, ref, blk=sib).wait_recv()

    def same_core(o):
        return ((chip + o) % nx) * 2 + core

    def share(name, ref):
        for o in range(1, nx):
            send((name, "x", o), ref.at[me], ref.at[me], blk=same_core(o))
        send((name, "c", 0), ref.at[me], ref.at[me], blk=sib)

    def pass_on(name, ref):
        for o in range(1, nx):
            block = ref.at[same_core(nx - o)]
            arrived((name, "x", o), block)
            send((name, "c", o), block, block, blk=sib)

    def take(name, ref):
        for o in range(nx):
            arrived((name, "c", o), ref.at[((chip + nx - o) % nx) * 2 + 1 - core])

    load_sizes.wait()
    load_picks.wait()
    size = sizes[0, 0]
    live_at = (lax.broadcasted_iota(jnp.int32, (width, width), 0) < size) & (
        lax.broadcasted_iota(jnp.int32, (width, width), 1) < size
    )
    load_wave.wait()
    pool[me] = jnp.where(live_at, wave_v[...].astype(F32), 0.0).astype(BF16)
    pl.semaphore_wait(
        barrier, nb - 1 + (sec > 0).astype(jnp.int32) + (sec < nsec - 1).astype(jnp.int32)
    )
    share("live", pool)
    load_left.wait()
    for o in range(1, nx):
        for j in range(pre):
            for c in range(2):
                channel = (((chip + o) % nx) * 2 + c) * per + j
                send(
                    ("left", o, j, c), left.at[channel], lpre.at[((o - 1) * pre + j) * 2 + c],
                    blk=same_core(o),
                )
    pass_on("live", pool)
    load_right.wait()
    take("live", pool)

    for t in range(channels):
        inner[:, t * width:(t + 1) * width] = dot(left[t], pool[picks[0, t]]).astype(BF16)
    total = dot(inner[...], right[...].reshape(channels * width, width))
    first = jnp.where(live_at, total, 0.0).astype(BF16)
    fpool[me] = first
    share("first", fpool)
    out1[...] = first

    first_f = fpool[me].astype(F32)
    first_t = jnp.transpose(first_f).astype(BF16)

    rounds = [(o, j) for o in list(range(1, nx)) + [0] for j in range(pre, per)]
    rounds += [(0, j) for j in range(pre)]

    def partial(o, j, c):
        channel = (((chip + o) % nx) * 2 + c) * per + j
        term = dot(first_t, dot(left[channel], fpool[me]).astype(BF16))
        if j < pre:
            for p in range(1, nx):
                lv = dot(lpre[((p - 1) * pre + j) * 2 + c], fpool[same_core(nx - p)]).astype(BF16)
                term = term + dot(tpre[p - 1], lv)
        return term.astype(BF16)

    def combine(r):
        o, j = rounds[r]
        arrived(("part", r), precv.at[r])
        both = mine[r].astype(F32) + precv[r].astype(F32)
        if o == 0:
            acc_at = j
            edge[acc_at] = both.astype(BF16)
        else:
            slot = (o - 1) * per + j
            rsend[slot] = both.astype(BF16)
            send(("rs", o, j), rsend.at[slot], rrecv.at[slot], blk=same_core(o))

    for r, (o, j) in enumerate(rounds):
        if j < pre and j == 0:
            pass_on("first", fpool)
            for p in range(1, nx):
                tpre[p - 1] = jnp.transpose(fpool[same_core(nx - p)].astype(F32)).astype(BF16)
                for i in range(pre):
                    for c in range(2):
                        slot = ((p - 1) * pre + i) * 2 + c
                        arrived(("left", p, i, c), lpre.at[slot])
        psend[r] = partial(o, j, 1 - core)
        send(("part", r), psend.at[r], precv.at[r], blk=sib)
        mine[r] = partial(o, j, core)
        if r == 0:
            squares = jnp.sum((first_f * first_f).reshape(width // 8, 8, width), axis=0)
            fold = squares[:, :128]
            for c in range(128, width, 128):
                fold = fold + squares[:, c:c + 128]
            meta[me, :8] = fold
            meta[me, 8:] = jnp.full((8, 128), (size * size).astype(F32), F32)
            for p in range(1, nb):
                send(("meta", p), meta.at[me], meta.at[me], blk=(me + p) % nb)
        if r >= 1:
            combine(r - 1)
    combine(len(rounds) - 1)

    if not pre:
        pass_on("first", fpool)
    for p in range(1, nb):
        arrived(("meta", p), meta.at[(me + nb - p) % nb])
    totals = jnp.sum(meta[...], axis=0)
    square_sum = jnp.sum(totals[:8], keepdims=True)
    count = jnp.sum(totals[8:], keepdims=True) * (1.0 / 1024)
    scale = lax.rsqrt(square_sum / count + 1e-06)
    factor = scale * scale * (1.0 / (width * math.sqrt(nb)))
    take("first", fpool)

    later = []

    def up(j):
        result = edge[j].astype(F32)
        for o in range(1, nx if j >= pre else 1):
            slot = (o - 1) * per + j
            arrived(("rs", o, j), rrecv.at[slot])
            result = result + rrecv[slot].astype(F32)
        edge[j] = (result * factor).astype(BF16)
        copy = remote(("up", j), edge.at[j], inc.at[me * per + j], sec=sec + 1)
        later.append(copy)

        @pl.when(sec < nsec - 1)
        def _():
            copy.start()

    inner_sends = []

    def spread(j):
        t = me * per + j
        block = inc.at[t]
        outs = [remote(("inc", j, "x", o), block, block, blk=same_core(o)) for o in range(1, nx)]
        outs.append(remote(("inc", j, "c", 0), block, block, blk=sib))
        inner_sends.extend(outs)

        @pl.when(sec > 0)
        def _():
            arrived(("up", j), block)
            for copy in outs:
                copy.start()

    def hand_on(j):
        pairs = []
        for o in range(1, nx):
            block = inc.at[same_core(nx - o) * per + j]
            pairs.append((o, block, remote(("inc", j, "c", o), block, block, blk=sib)))
        inner_sends.extend(copy for _, _, copy in pairs)

        @pl.when(sec > 0)
        def _():
            for o, block, copy in pairs:
                arrived(("inc", j, "x", o), block)
                copy.start()

    def second(j):
        result = acc[...] if j else None
        for c in (core, 1 - core):
            for o in range(nx):
                t = (((chip + nx - o) % nx) * 2 + c) * per + j
                if c is not core:

                    @pl.when(sec > 0)
                    def _():
                        arrived(("inc", j, "c", o), inc.at[t])

                left_two = (left[t].astype(F32) + inc[t].astype(F32)).astype(BF16)
                step = dot(dot(left_two, fpool[picks[0, t]]).astype(BF16), right[t])
                result = step if result is None else result + step
        acc[...] = result

    @pl.when(sec == 0)
    def _():
        inc[...] = jnp.zeros_like(inc)

    for tick in range(per + 4):
        if tick < per:
            up(tick)
        if 1 <= tick < per + 1:
            spread(tick - 1)
        if 2 <= tick < per + 2:
            hand_on(tick - 2)
        if 3 <= tick < per + 3:
            second(tick - 3)

    out2[...] = jnp.where(live_at, acc[...] * scale, 0.0).astype(BF16)

    for copy in sent:
        copy.wait_send()

    @pl.when(sec < nsec - 1)
    def _():
        for copy in later:
            copy.wait_send()

    @pl.when(sec > 0)
    def _():
        for copy in inner_sends:
            copy.wait_send()


def write_out(first, second, first_h, second_h, sem):
    copies = [
        pltpu.make_async_copy(first, first_h, sem.at[0]),
        pltpu.make_async_copy(second, second_h, sem.at[1]),
    ]
    for copy in copies:
        copy.start()
    for copy in copies:
        copy.wait()


def shards(nsec, nb, wave, left, right, picks, sizes):
    width = wave.shape[-1]
    channels = left.shape[2]
    nx = nb // 2
    per = channels // nb
    block = (width, width)
    copies = copies_between(nb, per)
    pre = ahead(nb, per)
    vmem = lambda *lead: pltpu.VMEM((*lead, *block), BF16)
    anywhere = pl.BlockSpec(memory_space=pltpu.HBM)
    out = pltpu.VMEM(block, BF16)
    first, second = pl.pallas_call(
        functools.partial(kernel, nsec, nb),
        out_shape=(out, out),
        in_specs=[anywhere] * 5,
        out_specs=(pl.BlockSpec(memory_space=pltpu.VMEM),) * 2,
        scratch_shapes=[
            pltpu.SMEM((1, channels), jnp.int32),
            pltpu.SMEM((1, 1), jnp.int32),
            vmem(),
            vmem(channels),
            vmem(channels),
            vmem(nb),
            vmem(nb),
            pltpu.VMEM((width, channels * width), BF16),
            vmem(nx * per),
            vmem(nx * per),
            vmem(nx * per),
            vmem((nx - 1) * per),
            vmem((nx - 1) * per),
            vmem(per),
            vmem(channels),
            pltpu.VMEM((nb, 16, 128), F32),
            pltpu.VMEM(block, F32),
            vmem(max(1, 2 * (nx - 1) * pre)),
            vmem(nx - 1),
            pltpu.SemaphoreType.DMA((5,)),
            pltpu.SemaphoreType.DMA((copies,)),
            pltpu.SemaphoreType.DMA((copies,)),
        ],
        compiler_params=pltpu.CompilerParams(
            collective_id=0, has_side_effects=True, vmem_limit_bytes=62 * 2**20
        ),
        cost_estimate=pl.CostEstimate(
            flops=12 * channels * width**3, bytes_accessed=4 * channels * width**2, transcendentals=0
        ),
    )(
        picks.reshape(1, channels),
        sizes.reshape(1, 1),
        wave.reshape(block),
        left.reshape(channels, *block),
        right.reshape(channels, *block),
    )
    result = jax.ShapeDtypeStruct(block, BF16)
    first, second = pl.pallas_call(
        write_out,
        out_shape=(result, result),
        in_specs=[pl.BlockSpec(memory_space=pltpu.VMEM)] * 2,
        out_specs=(pl.BlockSpec(memory_space=pl.ANY),) * 2,
        scratch_shapes=[pltpu.SemaphoreType.DMA((2,))],
        compiler_params=pltpu.CompilerParams(has_side_effects=True),
    )(*(pltpu.with_memory_space_constraint(x, pltpu.VMEM) for x in (first, second)))
    return first[None, None], second[None, None]


def solution(mesh):
    return jax.shard_map(
        functools.partial(shards, mesh.shape["sec"], mesh.shape["blk"]),
        mesh=mesh,
        in_specs=(
            P("sec", "blk", None, None),
            P("sec", "blk", None, None, None),
            P("sec", "blk", None, None, None),
            P("sec", "blk", None),
            P("sec", "blk"),
        ),
        out_specs=(P("sec", "blk", None, None), P("sec", "blk", None, None)),
        check_vma=False,
    )
```
